128 devices in a mesh: rep: 4 (over y_lo, core), fsdp: 32 (over x, y_hi, z).
Axes of the slice: x: 4, y: 4 (y_hi: 2, y_lo: 2; y = y_hi * 2 + y_lo), z: 4, core: 2. Of those that a mesh axis runs over, the one named last changes fastest.
Arguments:
- tokens: bfloat16 [65536, 16384], P(('rep', 'fsdp')), may hold values from -24 to 24
- cotangent: bfloat16 [65536, 512], P(('rep', 'fsdp')), may hold values from -0.0625 to 0.0625
- master: float32 [16384, 512], P('fsdp'), may hold values from -4 to 4
- moment1: float32 [16384, 512], P('fsdp'), may hold values from -3 to 3
- moment2: float32 [16384, 512], P('fsdp'), may hold values from 0.05 to 5
- owner: int32 [8192], replicated, may hold values from 0 to 127, as said below
Outputs:
- master_new: float32 [16384, 512], P('fsdp')
- moment1_new: float32 [16384, 512], P('fsdp')
- moment2_new: float32 [16384, 512], P('fsdp')
- upload: bfloat16 [16384, 2, 512], P(('rep', 'fsdp'))
The draws below stay inside these ranges and needn't reach their ends.
Inputs may be any that keep to these rules, and one draw needn't show every extreme that they name: For every shard s and device w, at most 4 blocks of shard s have owner w, and some device owns exactly 4 blocks of each shard.
All inputs are finite; a program needn't handle non-finite values.
Results may differ from the reference program's by a relative error of at most 0.015.
Values may be sent and summed in bfloat16 or wider, within the bound.
No kernel may reach another device: no remote copies, remote signals or barrier semaphores. Data moves between devices by JAX's collectives and lax.ppermute only.
A program may use at most 192 MiB of HBM per device.

```python
import math
import jax
import jax.numpy as jnp
from jax import lax

D = 16384
COLS = 512
TOK_DEV = 512
BLOCK_ROWS = 2
TOKENS = 65536
BLOCKS_SHARD = 256
CAPACITY = 4
N_REP = 4
N_FSDP = 32


def draw_owner(key, part):
    key = jax.random.fold_in(key, 7)
    per_row = BLOCKS_SHARD // N_REP
    half_count = N_FSDP // 2

    def one_shard(shard_key):
        count_key, forced_key, order_key, place_key = jax.random.split(shard_key, 4)
        counts = jax.random.randint(count_key, (N_REP, half_count), 0, CAPACITY + 1)
        forced = jax.random.randint(forced_key, (N_REP,), 0, half_count)
        columns = jnp.arange(half_count, dtype=jnp.int32)[None, :]
        counts = jnp.where(columns == forced[:, None], CAPACITY, counts)
        counts = jnp.concatenate([counts, CAPACITY - counts], axis=1).astype(jnp.int32)
        orders = jax.vmap(lambda row_key: jax.random.permutation(row_key, N_FSDP))(jax.random.split(order_key, N_REP))
        bounds = jnp.cumsum(counts, axis=1)
        within = jnp.arange(per_row, dtype=jnp.int32)
        position = jnp.sum((bounds[:, None, :] <= within[None, :, None]).astype(jnp.int32), axis=2)
        target = jnp.take_along_axis(orders.astype(jnp.int32), position, axis=1)
        owners = jnp.arange(N_REP, dtype=jnp.int32)[:, None] * N_FSDP + target
        placing = jax.random.permutation(place_key, BLOCKS_SHARD)
        return jnp.zeros((BLOCKS_SHARD,), jnp.int32).at[placing].set(owners.reshape(-1))
    return jax.vmap(one_shard)(jax.random.split(key, N_FSDP)).reshape(-1).astype(jnp.int32)


def raised(entries, rng, source, target, blocks, factor):
    def block_of(dim):
        return (jnp.arange(entries.shape[dim]) // (entries.shape[dim] // blocks)).reshape((-1,) + (1,) * (entries.ndim - 1 - dim))

    one_side = jax.random.permutation(rng, blocks)[block_of(target)]
    second = (block_of(target) + blocks // 2) % blocks
    return jnp.where((block_of(source) == one_side) | (block_of(source) == second), factor * entries, entries)


def level_of(rng, extent, pieces, least, high):
    def one(axis_at, parts):
        steps = jax.random.uniform(jax.random.fold_in(jax.random.fold_in(rng, 6), axis_at), (parts,), jnp.float32, least / len(pieces), high / len(pieces))
        return jnp.repeat(jnp.exp(steps), extent[axis_at] // parts).reshape((-1,) + (1,) * (len(extent) - axis_at - 1))

    factor_of = one(*pieces[0])
    for cut in pieces[1:]:
        factor_of = factor_of * one(*cut)
    return factor_of


def normal_values(stream_key, dims, spread, most, cuts=(), kind=jnp.bfloat16):
    entries = spread * jax.random.normal(stream_key, dims, jnp.float32)
    if cuts:
        entries = entries * level_of(stream_key, dims, cuts, -0.22, 0.18)
    return jnp.clip(entries, -most, most).astype(kind)


def heavy_noise(stream_key, dims, deviation, reach, cuts, heavy, held_as=jnp.bfloat16):
    values = deviation * jax.random.normal(stream_key, dims, jnp.float32)
    if cuts:
        values = values * level_of(stream_key, dims, cuts, -0.22, 0.18)
    return jnp.clip(raised(values, jax.random.fold_in(stream_key, 3), *heavy), -reach, reach).astype(held_as)


def setup_inputs(seed: int = 0) -> dict:
    arg_keys = jax.random.split(jax.random.key(seed), 7)
    return {
        "tokens": heavy_noise(arg_keys[0], (TOKENS, D), 1.0, 24.0, ((0, 128),), (0, 1, 128, 5.5)),
        "cotangent": normal_values(arg_keys[1], (TOKENS, COLS), ((TOK_DEV * N_REP * N_FSDP) ** -0.5), 0.0625, ((0, 128),)),
        "master": normal_values(arg_keys[2], (D, COLS), 0.5, 4.0, ((0, 32),), jnp.float32),
        "moment1": normal_values(arg_keys[3], (D, COLS), 0.3, 3.0, ((0, 32),), jnp.float32),
        "moment2": jnp.clip(jnp.exp(math.log(5.0) - 4.6051702 * jax.random.uniform(arg_keys[4], (D, COLS), jnp.float32) ** level_of(arg_keys[4], (D, COLS), ((0, 32),), -0.2, 0.2)), 0.05, 5.0),
        "owner": draw_owner(jax.random.fold_in(arg_keys[6], 71), 0),
    }


bias_first = 1.0 - 0.9 ** 10
bias_second = 1.0 - 0.95 ** 10

def adam_update(grad, master, moment1, moment2):
    first = 0.9 * moment1 + 0.1 * grad
    second = 0.95 * moment2 + 0.05 * grad * grad
    update = first / bias_first / (jnp.sqrt(second / bias_second) + 1e-08)
    return (master - 0.05 * (update + 0.1 * master), first, second)

def block_ranks(owners):
    equal = owners[:, None] == owners[None, :]
    places = jnp.arange(owners.shape[0], dtype=jnp.int32)
    earlier = places[None, :] < places[:, None]
    return lax.optimization_barrier(jnp.sum(jnp.logical_and(equal, earlier), axis=1)).astype(jnp.int32)

def reference(tokens, cotangent, master, moment1, moment2, owner):
    grad = lax.dot_general(tokens, cotangent, (((0,), (0,)), ((), ())), preferred_element_type=jnp.float32)
    master_new, moment1_new, moment2_new = adam_update(grad, master, moment1, moment2)
    weight = master_new.astype(jnp.bfloat16)
    blocks = weight.reshape(N_FSDP * BLOCKS_SHARD, BLOCK_ROWS, COLS)
    owner_grid = owner.reshape(N_FSDP, BLOCKS_SHARD)
    ranks = lax.map(block_ranks, owner_grid)
    shard_ids = jnp.arange(N_FSDP, dtype=jnp.int32)[:, None]
    slots = owner_grid * (N_FSDP * CAPACITY) + shard_ids * CAPACITY + ranks
    upload = jnp.zeros((N_REP * N_FSDP * N_FSDP * CAPACITY, BLOCK_ROWS, COLS), jnp.bfloat16)
    upload = upload.at[slots.reshape(-1).astype(jnp.int32)].set(blocks)
    return (master_new, moment1_new, moment2_new, upload)
```

```python
import functools

import jax
import jax.numpy as jnp
from jax import lax
from jax.experimental import pallas as pl
from jax.experimental.pallas import tpu as pltpu
from jax.sharding import PartitionSpec as P

BLOCK_ROWS = 2
AXES = ("rep", "fsdp")
SIDE = 4
PARTS = ((0, 176), (176, 256))

bias_first = 1.0 - 0.9**10
bias_second = 1.0 - 0.95**10

ORDERS = (((0, 1, 2), (1, 2, 0)), ((2, 0, 1), (2, 0, 1)))


def coords(index):
    rep, fsdp = divmod(index, 32)
    y_lo, core = divmod(rep, 2)
    x, rest = divmod(fsdp, 8)
    y_hi, z = divmod(rest, 4)
    return x, y_hi * 2 + y_lo, z, core


def index_of(x, y, z, core):
    return ((y % 2) * 2 + core) * 32 + x * 8 + (y // 2) * 4 + z


def ring_pairs(part, stage, distance):
    pairs = []
    for device in range(128):
        place = list(coords(device))
        axis = ORDERS[part][place[3]][stage]
        place[axis] = (place[axis] + distance) % SIDE
        pairs.append((device, index_of(*place)))
    return pairs


def rep_pairs(bit):
    return [(device, (((device // 32) ^ bit) * 32) + device % 32) for device in range(128)]


def send(value, pairs):
    return lax.ppermute(value, AXES, pairs)


def matmul_body(rows, count, has_sum, table, cot, *refs):
    first, last = rows
    tokens = refs[:count]
    out = refs[-1]
    left = cot[first:last, :]
    for at in range(count):
        total = jnp.dot(left, tokens[at][...], preferred_element_type=jnp.float32)
        if has_sum:
            total = total + refs[count][at].astype(jnp.float32)
        out[at] = total.astype(jnp.bfloat16)


def pieces(table, cot_t, tokens, part, side, distance, received=None):
    rows = PARTS[part]
    width = rows[1] - rows[0]
    depth, lanes = tokens.shape[0], 256
    base = 12 * (part * 2 + side)

    def token_map(at, step, table):
        return (0, table[base + distance] + table[base + 4 + step] + table[base + 8 + at])

    in_specs = [pl.BlockSpec((256, depth), lambda step, table: (table[48 + side], 0))]
    in_specs += [
        pl.BlockSpec((depth, lanes), functools.partial(token_map, at)) for at in range(SIDE)
    ]
    operands = [table, cot_t] + [tokens] * SIDE
    piece_spec = pl.BlockSpec((SIDE, width, lanes), lambda step, table: (step, 0, 0))
    if received is not None:
        in_specs.append(piece_spec)
        operands.append(received)
    return pl.pallas_call(
        functools.partial(matmul_body, rows, SIDE, received is not None),
        out_shape=jax.ShapeDtypeStruct((SIDE * SIDE, width, lanes), jnp.bfloat16),
        grid_spec=pltpu.PrefetchScalarGridSpec(
            num_scalar_prefetch=1, grid=(SIDE,), in_specs=in_specs, out_specs=piece_spec
        ),
        compiler_params=pltpu.CompilerParams(vmem_limit_bytes=24 * 1024 * 1024),
        cost_estimate=pl.CostEstimate(
            flops=2 * width * depth * lanes * 16, bytes_accessed=6_000_000, transcendentals=0
        ),
    )(*operands)


def adam_body(table, own, other, master, moment1, moment2, master_new, first_new, second_new, weight):
    mine = own[0].T.astype(jnp.float32)
    theirs = other[0].T.astype(jnp.float32)
    is_first = table[50] == 0
    grad = jnp.concatenate(
        [jnp.where(is_first, mine, theirs), jnp.where(is_first, theirs, mine)], axis=1
    )
    first = 0.9 * moment1[...] + 0.1 * grad
    second = 0.95 * moment2[...] + 0.05 * grad * grad
    update = first / bias_first / (jnp.sqrt(second / bias_second) + 1e-08)
    new = master[...] - 0.05 * (update + 0.1 * master[...])
    master_new[...] = new
    first_new[...] = first
    second_new[...] = second
    weight[...] = new.astype(jnp.bfloat16)


def adam(table, own, other, master, moment1, moment2):
    rows, columns = master.shape
    half = rows // 2
    grad_spec = pl.BlockSpec((1, columns // 2, half), lambda i, table: (i ^ table[51], 0, 0))
    row_spec = pl.BlockSpec((half, columns), lambda i, table: (i, 0))
    return pl.pallas_call(
        adam_body,
        out_shape=[jax.ShapeDtypeStruct((rows, columns), jnp.float32)] * 3
        + [jax.ShapeDtypeStruct((rows, columns), jnp.bfloat16)],
        grid_spec=pltpu.PrefetchScalarGridSpec(
            num_scalar_prefetch=1,
            grid=(2,),
            in_specs=[grad_spec, grad_spec, row_spec, row_spec, row_spec],
            out_specs=[row_spec] * 4,
        ),
        compiler_params=pltpu.CompilerParams(vmem_limit_bytes=32 * 1024 * 1024),
        cost_estimate=pl.CostEstimate(
            flops=20 * rows * columns, bytes_accessed=28 * rows * columns, transcendentals=0
        ),
    )(table, own, other, master, moment1, moment2)


def position_table():
    rep, fsdp = lax.axis_index("rep"), lax.axis_index("fsdp")
    core, y_lo = rep % 2, rep // 2
    place = (fsdp // 8, (fsdp // 4) % 2 * 2 + y_lo, fsdp % 4)
    away = jnp.arange(SIDE, dtype=jnp.int32)
    steps = []
    for axis in range(3):
        at = (place[axis] + away) % SIDE
        steps.append((at * 16, (at // 2) * 8 + at % 2, at * 2)[axis])
    rows = []
    for part in range(2):
        for side in range(2):
            target = core ^ side
            rows.append(
                jnp.where(
                    target == 0,
                    jnp.concatenate([steps[axis] for axis in ORDERS[part][0]]),
                    jnp.concatenate([steps[axis] for axis in ORDERS[part][1]]),
                )
            )
    rest = jnp.stack([core, 1 - core, core, y_lo]).astype(jnp.int32)
    return jnp.concatenate(rows + [rest]).astype(jnp.int32)


def reduce_part(table, cot_t, tokens, part):
    own = {}
    for distance in (1, 3, 2, 0):
        other = pieces(table, cot_t, tokens, part, 1, distance)
        arrived = send(other, rep_pairs(1))
        own[distance] = pieces(table, cot_t, tokens, part, 0, distance, arrived)
    width = PARTS[part][1] - PARTS[part][0]
    groups = [own[distance].reshape(SIDE, SIDE, width, 256) for distance in range(SIDE)]
    for stage in range(3):
        arrived = [groups[0]]
        for distance in (1, 3, 2):
            arrived.append(send(groups[distance], ring_pairs(part, stage, distance)))
        if stage == 2:
            return sum(value.astype(jnp.float32) for value in arrived).astype(jnp.bfloat16)
        groups = [
            sum(value[at].astype(jnp.float32) for value in arrived).astype(jnp.bfloat16)
            for at in range(SIDE)
        ]


def per_device(tokens, cotangent, master, moment1, moment2, owner):
    fsdp_count = lax.axis_size("fsdp")
    rep_count = lax.axis_size("rep")
    shard_rows = master.shape[0]
    columns = master.shape[1]
    table = position_table()
    cot_t = cotangent.T
    mine = jnp.concatenate([reduce_part(table, cot_t, tokens, part) for part in range(2)], axis=0)
    beside = send(mine, rep_pairs(2))
    own = jnp.stack([mine, beside])
    other = send(own, rep_pairs(1))
    master_new, moment1_new, moment2_new, weight = adam(
        table, own, other, master, moment1, moment2
    )
    local_blocks = shard_rows // BLOCK_ROWS
    capacity = 2 * local_blocks // (rep_count * fsdp_count)
    blocks = weight.reshape(local_blocks, BLOCK_ROWS * columns)
    owners = lax.dynamic_slice_in_dim(owner, lax.axis_index("fsdp") * local_blocks, local_blocks)
    in_row = owners // fsdp_count == lax.axis_index("rep")
    target = owners % fsdp_count
    places = jnp.arange(local_blocks, dtype=jnp.int32)
    equal = owners[:, None] == owners[None, :]
    earlier = places[None, :] < places[:, None]
    ranks = jnp.sum(jnp.logical_and(equal, earlier), axis=1)
    slots = target * capacity + ranks
    slot_ids = jnp.arange(fsdp_count * capacity, dtype=jnp.int32)
    selector = jnp.logical_and(slot_ids[:, None] == slots[None, :], in_row[None, :]).astype(
        jnp.bfloat16
    )
    outgoing = jnp.dot(selector, blocks, preferred_element_type=jnp.float32).astype(jnp.bfloat16)
    outgoing = outgoing.reshape(fsdp_count, capacity, BLOCK_ROWS, columns)
    received = lax.all_to_all(outgoing, "fsdp", split_axis=0, concat_axis=0, tiled=True)
    upload = received.reshape(fsdp_count * capacity, BLOCK_ROWS, columns)
    return (master_new, moment1_new, moment2_new, upload)


def solution(mesh):
    placed = (
        P(("rep", "fsdp"), None),
        P(("rep", "fsdp"), None),
        P("fsdp", None),
        P("fsdp", None),
        P("fsdp", None),
        P(),
    )
    return jax.shard_map(
        per_device,
        mesh=mesh,
        in_specs=placed,
        out_specs=(
            P("fsdp", None),
            P("fsdp", None),
            P("fsdp", None),
            P(("rep", "fsdp"), None, None),
        ),
        check_vma=False,
    )
```

```python
import jax
import jax.numpy as jnp
from jax import lax
from jax.experimental import pallas as pl
from jax.experimental.pallas import tpu as pltpu
from jax.sharding import PartitionSpec as P

BLOCK_ROWS = 2
AXES = ("rep", "fsdp")
SIDE = 4
PARTS = ((0, 352), (352, 512))

bias_first = 1.0 - 0.9**10
bias_second = 1.0 - 0.95**10

ORDERS = (((0, 1, 2), (1, 2, 0)), ((2, 0, 1), (2, 0, 1)))


def coords(index):
    rep, fsdp = divmod(index, 32)
    y_lo, core = divmod(rep, 2)
    x, rest = divmod(fsdp, 8)
    y_hi, z = divmod(rest, 4)
    return x, y_hi * 2 + y_lo, z, core


def index_of(x, y, z, core):
    return ((y % 2) * 2 + core) * 32 + x * 8 + (y // 2) * 4 + z


def ring_pairs(part, stage, distance):
    pairs = []
    for device in range(128):
        place = list(coords(device))
        axis = ORDERS[part][place[3]][stage]
        place[axis] = (place[axis] + distance) % SIDE
        pairs.append((device, index_of(*place)))
    return pairs


def swap_pairs(part, odd):
    pairs = []
    for device in range(128):
        place = list(coords(device))
        axis = ORDERS[part][place[3]][0]
        place[axis] = (((place[axis] + odd) ^ 1) - odd) % SIDE
        pairs.append((device, index_of(*place)))
    return pairs


def rep_pairs(bit):
    return [(device, (((device // 32) ^ bit) * 32) + device % 32) for device in range(128)]


def send(value, pairs):
    return lax.ppermute(value, AXES, pairs)


def split_body(cot, tokens, *refs):
    own, other = refs[:4], refs[4:8]
    cot_t, held, kept, in_sem, cot_sem, sem = refs[8:]
    steps, _, lanes = held.shape
    rep, fsdp = lax.axis_index("rep"), lax.axis_index("fsdp")
    core, y_lo = lax.rem(rep, 2), rep // 2
    place = (fsdp // 8, lax.rem(fsdp // 4, 2) * 2 + y_lo, lax.rem(fsdp, 4))
    count = SIDE * SIDE
    ahead = 2
    first_rows = 2 * count * (PARTS[0][1] - PARTS[0][0]) // 2

    def fetch(step):
        columns = pl.ds(pl.multiple_of(step * lanes, lanes), lanes)
        return pltpu.make_async_copy(tokens.at[:, columns], held.at[step], in_sem.at[step])

    def drain(slot):
        pltpu.make_async_copy(kept.at[slot], kept.at[slot], sem.at[slot]).wait()

    def group(axis, away):
        parity = lax.rem(place[axis], 2)
        is_even = away == 1 + 2 * parity
        is_odd = away == 3 - 2 * parity
        is_far = away == 2
        one = lambda flag: jnp.where(flag, 1, 0)
        return (
            (one(is_even) + one(is_far), one(is_far) + one(is_odd)),
            (one(is_odd) + one(is_far), one(is_far) + one(is_even)),
        )

    cot_copy = pltpu.make_async_copy(cot, cot_t.at[1], cot_sem)
    cot_copy.start()
    for step in range(ahead):
        fetch(step).start()
    cot_copy.wait()
    cot_t[0] = cot_t[1].T

    def one_step(step, carry):
        slot = lax.rem(step, 2)
        fetch(step).wait()

        @pl.when(step + ahead < steps)
        def _():
            fetch(step + ahead).start()

        @pl.when(step >= 2)
        def _():
            drain(slot)

        total = jnp.dot(cot_t[0], held[step], preferred_element_type=jnp.float32)
        for at in range(count):
            kept[slot, at] = total[:, at * 128 : (at + 1) * 128].astype(jnp.bfloat16)

        away_x = lax.rem(step // 2 - place[0] + SIDE, SIDE)
        groups_x = group(0, away_x)
        for z in range(SIDE):
            away_z = lax.rem(z - place[2] + SIDE, SIDE)
            groups_z = group(2, away_z)
            for low in range(2):
                away_y = lax.rem(lax.rem(step, 2) * 2 + low - place[1] + SIDE, SIDE)
                groups_y = group(1, away_y)
                for side, arrays in ((1, other), (0, own)):
                    target = core if side == 0 else 1 - core
                    source = z * 4 + low * 2 + target
                    is_first = target == 0
                    rest_a = jnp.where(is_first, away_y * 4 + away_z, away_z * 4 + away_x)
                    rest_b = away_x * 4 + away_y
                    for odd in range(2):
                        for part in range(2):
                            low_column, high_column = PARTS[part]
                            width = (high_column - low_column) // 2
                            column = low_column + odd * width
                            if part == 0:
                                sent = jnp.where(is_first, groups_x[odd][0], groups_y[odd][0])
                                second = jnp.where(is_first, groups_x[odd][1], groups_y[odd][1])
                                row = (second * count + rest_a) * width
                            else:
                                sent, second = groups_z[odd]
                                row = first_rows + (second * count + rest_b) * width
                            row = pl.multiple_of(row, 16)
                            for array, flag in ((arrays[odd], 1), (arrays[2 + odd], 0)):

                                @pl.when(sent == flag)
                                def _(
                                    array=array, source=source, column=column, width=width, row=row
                                ):
                                    pltpu.make_async_copy(
                                        kept.at[slot, source, pl.ds(column, width)],
                                        array.at[pl.ds(row, width)],
                                        sem.at[slot],
                                    ).start()

        return carry

    lax.fori_loop(0, steps, one_step, 0)
    drain(0)
    drain(1)


def split_sums(tokens, cotangent):
    depth, rows = tokens.shape
    columns = cotangent.shape[1]
    lanes = 16 * 128
    steps = rows // lanes
    count = SIDE * SIDE
    sums = jax.ShapeDtypeStruct((count * columns, 128), jnp.bfloat16)
    anywhere = pl.BlockSpec(memory_space=pl.ANY)
    results = pl.pallas_call(
        split_body,
        out_shape=[sums] * 8,
        in_specs=[anywhere] * 2,
        out_specs=[anywhere] * 8,
        scratch_shapes=[
            pltpu.VMEM((2, columns, depth), jnp.bfloat16),
            pltpu.VMEM((steps, depth, lanes), jnp.bfloat16),
            pltpu.VMEM((2, count, columns, 128), jnp.bfloat16),
            pltpu.SemaphoreType.DMA((steps,)),
            pltpu.SemaphoreType.DMA,
            pltpu.SemaphoreType.DMA((2,)),
        ],
        compiler_params=pltpu.CompilerParams(vmem_limit_bytes=56 * 1024 * 1024),
        cost_estimate=pl.CostEstimate(
            flops=2 * depth * rows * columns, bytes_accessed=4 * depth * rows, transcendentals=0
        ),
    )(cotangent, tokens)
    return results[:4], results[4:]


def updated(grad, master, moment1, moment2):
    first = 0.9 * moment1 + 0.1 * grad
    second = 0.95 * moment2 + 0.05 * grad * grad
    update = first / bias_first / (jnp.sqrt(second / bias_second) + 1e-08)
    return master - 0.05 * (update + 0.1 * master), first, second


def rep_grad(own, other, at):
    rep = lax.axis_index("rep")
    core, y_lo = lax.rem(rep, 2), rep // 2
    index = y_lo if at // 2 == 0 else 1 - y_lo
    piece = jnp.where(core == at % 2, own[index], other[index])
    return piece.T.astype(jnp.float32)


def weight_body(own, other, master, moment1, moment2, selector, outgoing, weight):
    for at in range(4):
        rows = slice(at * 128, (at + 1) * 128)
        new, _, _ = updated(rep_grad(own, other, at), master[rows], moment1[rows], moment2[rows])
        weight[rows] = new.astype(jnp.bfloat16)
    chosen = jnp.dot(selector[...], weight[...], preferred_element_type=jnp.float32)
    outgoing[...] = chosen.astype(jnp.bfloat16).reshape(outgoing.shape)


def adam_body(own, other, master, moment1, moment2, *refs):
    outs, kept, sem = refs[:3], refs[3:6], refs[6]
    copies = []
    for at in range(4):
        rows = slice(at * 128, (at + 1) * 128)
        values = updated(rep_grad(own, other, at), master[rows], moment1[rows], moment2[rows])
        for k in range(3):
            kept[k][rows] = values[k]
            copy = pltpu.make_async_copy(
                kept[k].at[pl.ds(at * 128, 128)], outs[k].at[pl.ds(at * 128, 128)], sem.at[k, at]
            )
            copy.start()
            copies.append(copy)
    for copy in copies:
        copy.wait()


def adam(own, other, master, moment1, moment2, selector):
    rows, columns = master.shape
    size = rows * columns
    params = pltpu.CompilerParams(vmem_limit_bytes=32 * 1024 * 1024)
    vmem = pl.BlockSpec(memory_space=pltpu.VMEM)
    outgoing = pl.pallas_call(
        weight_body,
        out_shape=jax.ShapeDtypeStruct(
            (selector.shape[0] // BLOCK_ROWS, BLOCK_ROWS, columns), jnp.bfloat16
        ),
        in_specs=[vmem] * 6,
        out_specs=vmem,
        scratch_shapes=[pltpu.VMEM((rows, columns), jnp.bfloat16)],
        compiler_params=params,
        cost_estimate=pl.CostEstimate(
            flops=20 * size, bytes_accessed=14 * size, transcendentals=0
        ),
    )(own, other, master, moment1, moment2, selector)
    state = pl.pallas_call(
        adam_body,
        out_shape=[jax.ShapeDtypeStruct((rows, columns), jnp.float32)] * 3,
        in_specs=[vmem] * 5,
        out_specs=[pl.BlockSpec(memory_space=pl.ANY)] * 3,
        scratch_shapes=[pltpu.VMEM((rows, columns), jnp.float32)] * 3
        + [pltpu.SemaphoreType.DMA((3, 4))],
        compiler_params=params,
        cost_estimate=pl.CostEstimate(
            flops=20 * size, bytes_accessed=26 * size, transcendentals=0
        ),
    )(own, other, master, moment1, moment2)
    return outgoing, state


def add(values):
    return sum(value.astype(jnp.float32) for value in values).astype(jnp.bfloat16)


def after(value, *earlier):
    return lax.optimization_barrier((value, *earlier))[0]


def summed(own, other, early):
    count = SIDE * SIDE
    halves = [(last - first) // 2 for first, last in PARTS]
    cut = 2 * count * halves[0]
    rows = (slice(0, cut), slice(cut, None))
    beside = [send(other[odd], rep_pairs(1)) for odd in range(2)]
    beside += [send(after(other[2 + odd], beside[odd]), rep_pairs(1)) for odd in range(2)]
    came = {}
    for odd in range(2):
        both = after(beside[odd], *early)
        for part in range(2):
            value = add([own[odd][rows[part]], both[rows[part]]])
            came[part, odd] = send(value, swap_pairs(part, odd))
    near = {}
    for odd in range(2):
        for part in range(2):
            whole = add([own[2 + odd][rows[part]], beside[2 + odd][rows[part]], came[part, odd]])
            middle = whole.shape[0] // 2
            got = send(whole[middle:], swap_pairs(part, 1 - odd))
            near[part, odd] = (whole[:middle], got)
    values = []
    for part in range(2):
        shape = (SIDE, SIDE, halves[part], 128)
        pairs = [[value.reshape(shape) for value in near[part, odd]] for odd in range(2)]
        sums = [jnp.stack([add([v[at] for v in pair]) for pair in pairs]) for at in range(SIDE)]
        values.append([sums[0]] + [send(sums[at], ring_pairs(part, 1, at)) for at in (1, 3, 2)])
    mine = []
    for part in range(2):
        sums = [add([value[:, at] for value in values[part]]) for at in range(SIDE)]
        got = [sums[0]] + [send(sums[at], ring_pairs(part, 2, at)) for at in (1, 3, 2)]
        mine.append(add(got).reshape(2 * halves[part], 128))
    return jnp.concatenate(mine, axis=0)


def select_blocks(owner, local_blocks, capacity, fsdp_count):
    owners = lax.dynamic_slice_in_dim(owner, lax.axis_index("fsdp") * local_blocks, local_blocks)
    in_row = owners // fsdp_count == lax.axis_index("rep")
    target = owners % fsdp_count
    places = jnp.arange(local_blocks, dtype=jnp.int32)
    equal = owners[:, None] == owners[None, :]
    earlier = places[None, :] < places[:, None]
    ranks = jnp.sum(jnp.logical_and(equal, earlier), axis=1).astype(jnp.int32)
    slots = jnp.where(in_row, target * capacity + ranks, -1)
    row_slots = jnp.repeat(slots, BLOCK_ROWS) * BLOCK_ROWS + jnp.tile(
        jnp.arange(BLOCK_ROWS, dtype=jnp.int32), local_blocks
    )
    slot_rows = jnp.arange(fsdp_count * capacity * BLOCK_ROWS, dtype=jnp.int32)
    return (slot_rows[:, None] == row_slots[None, :]).astype(jnp.bfloat16)


def per_device(tokens, cotangent, master, moment1, moment2, owner):
    fsdp_count = lax.axis_size("fsdp")
    rep_count = lax.axis_size("rep")
    shard_rows = master.shape[0]
    columns = master.shape[1]
    local_blocks = shard_rows // BLOCK_ROWS
    capacity = 2 * local_blocks // (rep_count * fsdp_count)
    selector = select_blocks(owner, local_blocks, capacity, fsdp_count)
    mine = summed(*split_sums(tokens, cotangent), [selector])
    beside = send(mine, rep_pairs(2))
    own = jnp.stack([mine, beside])
    other = send(own, rep_pairs(1))
    outgoing, state = adam(own, other, master, moment1, moment2, selector)
    outgoing = outgoing.reshape(fsdp_count, capacity, BLOCK_ROWS, columns)
    received = lax.all_to_all(outgoing, "fsdp", split_axis=0, concat_axis=0, tiled=True)
    upload = received.reshape(fsdp_count * capacity, BLOCK_ROWS, columns)
    return (*state, upload)


def solution(mesh):
    placed = (
        P(("rep", "fsdp"), None),
        P(("rep", "fsdp"), None),
        P("fsdp", None),
        P("fsdp", None),
        P("fsdp", None),
        P(),
    )
    return jax.shard_map(
        per_device,
        mesh=mesh,
        in_specs=placed,
        out_specs=(
            P("fsdp", None),
            P("fsdp", None),
            P("fsdp", None),
            P(("rep", "fsdp"), None, None),
        ),
        check_vma=False,
    )
```

```python
import functools

import jax
import jax.numpy as jnp
from jax import lax
from jax.experimental import pallas as pl
from jax.experimental.pallas import tpu as pltpu
from jax.sharding import PartitionSpec as P

BLOCK_ROWS = 2
AXES = ("rep", "fsdp")
SIDE = 4

bias_first = 1.0 - 0.9**10
bias_second = 1.0 - 0.95**10

ORDERS = ((0, 1, 2), (1, 2, 0))


def coords(index):
    rep, fsdp = divmod(index, 32)
    y_lo, core = divmod(rep, 2)
    x, rest = divmod(fsdp, 8)
    y_hi, z = divmod(rest, 4)
    return x, y_hi * 2 + y_lo, z, core


def index_of(x, y, z, core):
    return ((y % 2) * 2 + core) * 32 + x * 8 + (y // 2) * 4 + z


def ring_pairs(stage, distance):
    pairs = []
    for device in range(128):
        place = list(coords(device))
        axis = ORDERS[place[3]][stage]
        place[axis] = (place[axis] + distance) % SIDE
        pairs.append((device, index_of(*place)))
    return pairs


def swap_pairs(odd):
    pairs = []
    for device in range(128):
        place = list(coords(device))
        axis = ORDERS[place[3]][0]
        place[axis] = (((place[axis] + odd) ^ 1) - odd) % SIDE
        pairs.append((device, index_of(*place)))
    return pairs


def rep_pairs(bit):
    return [(device, (((device // 32) ^ bit) * 32) + device % 32) for device in range(128)]


def send(value, pairs):
    return lax.ppermute(value, AXES, pairs)


def split_body(groups, cot, tokens, *refs):
    outs, (cot_t, held, kept, in_sem, cot_sem, sem) = refs[:-6], refs[-6:]
    columns = cot.shape[1]
    count = SIDE * SIDE
    rep, fsdp = lax.axis_index("rep"), lax.axis_index("fsdp")
    core, y_lo = lax.rem(rep, 2), rep // 2
    place = (fsdp // 8, lax.rem(fsdp // 4, 2) * 2 + y_lo, lax.rem(fsdp, 4))

    def fetch(at):
        side, half, is_sent = groups[at]
        target = core if side == 0 else 1 - core
        is_first = target == 0
        parity = lax.rem(jnp.where(is_first, place[0], place[1]), 2)
        even, odd = 1 + 2 * parity, 3 - 2 * parity
        distances = (odd if half else even, 2) if is_sent else (0, even if half else odd)
        tile = 0
        for one in distances:
            for two in (half, half + 2):
                for three in range(SIDE):
                    x = lax.rem(place[0] + jnp.where(is_first, one, three), SIDE)
                    y = lax.rem(place[1] + jnp.where(is_first, two, one), SIDE)
                    z = lax.rem(place[2] + jnp.where(is_first, three, two), SIDE)
                    lane = (x * 8 + (y // 2) * 4 + z) * 512 + lax.rem(y, 2) * 256 + target * 128
                    pltpu.make_async_copy(
                        tokens.at[:, pl.ds(pl.multiple_of(lane, 128), 128)],
                        held.at[at, :, pl.ds(tile * 128, 128)],
                        in_sem.at[at],
                    ).start()
                    tile += 1

    cot_copy = pltpu.make_async_copy(cot, cot_t.at[1], cot_sem)
    cot_copy.start()
    fetch(0)
    fetch(1)
    cot_copy.wait()
    cot_t[0] = cot_t[1].T
    copies = []
    done = 0
    for at in range(len(groups)):
        pltpu.make_async_copy(held.at[at], held.at[at], in_sem.at[at]).wait()
        if at + 2 < len(groups):
            fetch(at + 2)
        total = jnp.dot(cot_t[0], held[at], preferred_element_type=jnp.float32)
        parts = 1 if groups[at][2] else 2
        per_part = count // parts
        rows = per_part * columns
        for tile in range(count):
            piece = total[:, tile * 128 : (tile + 1) * 128].astype(jnp.bfloat16)
            part, index = divmod(tile, per_part)
            if groups[at][0] == 0:
                outs[done + part][index * columns : (index + 1) * columns] = piece
            else:
                kept[at, tile * columns : (tile + 1) * columns] = piece
        for part in range(parts):
            if groups[at][0] == 1:
                copy = pltpu.make_async_copy(
                    kept.at[at, pl.ds(part * rows, rows)], outs[done], sem.at[done]
                )
                copy.start()
                copies.append(copy)
            done += 1
    for copy in copies:
        copy.wait()


def split_sums(tokens, cotangent, groups):
    depth = tokens.shape[0]
    columns = cotangent.shape[1]
    rows = SIDE * SIDE * columns
    outs, specs = [], []
    for side, _, is_sent in groups:
        sizes = [rows] if is_sent else [rows // 2] * 2
        for size in sizes:
            place = pltpu.HBM if side else pltpu.VMEM
            outs.append(place((size, 128), jnp.bfloat16))
            specs.append(pl.BlockSpec(memory_space=pl.ANY if side else pltpu.VMEM))
    leaving = max(1, sum(side for side, _, _ in groups))
    return pl.pallas_call(
        functools.partial(split_body, groups),
        out_shape=outs,
        in_specs=[pl.BlockSpec(memory_space=pl.ANY)] * 2,
        out_specs=specs,
        scratch_shapes=[
            pltpu.VMEM((2, columns, depth), jnp.bfloat16),
            pltpu.VMEM((len(groups), depth, SIDE * SIDE * 128), jnp.bfloat16),
            pltpu.VMEM((leaving, rows, 128), jnp.bfloat16),
            pltpu.SemaphoreType.DMA((len(groups),)),
            pltpu.SemaphoreType.DMA,
            pltpu.SemaphoreType.DMA((len(outs),)),
        ],
        compiler_params=pltpu.CompilerParams(vmem_limit_bytes=32 * 1024 * 1024),
        cost_estimate=pl.CostEstimate(
            flops=2 * depth * rows * 128 * len(groups),
            bytes_accessed=512 * rows * len(groups),
            transcendentals=0,
        ),
    )(
        pltpu.with_memory_space_constraint(cotangent, pltpu.HBM),
        pltpu.with_memory_space_constraint(tokens, pltpu.HBM),
    )


def updated(grad, master, moment1, moment2):
    first = 0.9 * moment1 + 0.1 * grad
    second = 0.95 * moment2 + 0.05 * grad * grad
    update = first / bias_first / (jnp.sqrt(second / bias_second) + 1e-08)
    return master - 0.05 * (update + 0.1 * master), first, second


def rep_grad(own, other, at):
    rep = lax.axis_index("rep")
    core, y_lo = lax.rem(rep, 2), rep // 2
    index = y_lo if at // 2 == 0 else 1 - y_lo
    piece = jnp.where(core == at % 2, own[index], other[index])
    return piece.T.astype(jnp.float32)


def weight_body(own, other, master, moment1, moment2, selector, outgoing, weight):
    for at in range(4):
        rows = slice(at * 128, (at + 1) * 128)
        new, _, _ = updated(rep_grad(own, other, at), master[rows], moment1[rows], moment2[rows])
        weight[rows] = new.astype(jnp.bfloat16)
    outgoing[...] = jnp.dot(
        selector[...], weight[...], preferred_element_type=jnp.float32
    ).astype(jnp.bfloat16)


def unpack_body(rows, blocks):
    blocks[...] = rows[...].reshape(blocks.shape)


def unpacked(rows, block_rows):
    vmem = pl.BlockSpec(memory_space=pltpu.VMEM)
    shape = (rows.shape[0] // block_rows, block_rows, rows.shape[1])
    return pl.pallas_call(
        unpack_body,
        out_shape=jax.ShapeDtypeStruct(shape, rows.dtype),
        in_specs=[vmem],
        out_specs=vmem,
    )(rows)


def adam_body(own, other, master, moment1, moment2, *refs):
    outs, kept, sem = refs[:3], refs[3:6], refs[6]
    copies = []
    for at in range(4):
        rows = slice(at * 128, (at + 1) * 128)
        values = updated(rep_grad(own, other, at), master[rows], moment1[rows], moment2[rows])
        for k in range(3):
            kept[k][rows] = values[k]
            copy = pltpu.make_async_copy(
                kept[k].at[pl.ds(at * 128, 128)], outs[k].at[pl.ds(at * 128, 128)], sem.at[k, at]
            )
            copy.start()
            copies.append(copy)
    for copy in copies:
        copy.wait()


def adam(own, other, master, moment1, moment2, selector):
    rows, columns = master.shape
    size = rows * columns
    params = pltpu.CompilerParams(vmem_limit_bytes=12 * 1024 * 1024)
    vmem = pl.BlockSpec(memory_space=pltpu.VMEM)
    outgoing = pl.pallas_call(
        weight_body,
        out_shape=jax.ShapeDtypeStruct((selector.shape[0], columns), jnp.bfloat16),
        in_specs=[vmem] * 6,
        out_specs=vmem,
        scratch_shapes=[pltpu.VMEM((rows, columns), jnp.bfloat16)],
        compiler_params=params,
        cost_estimate=pl.CostEstimate(
            flops=20 * size, bytes_accessed=14 * size, transcendentals=0
        ),
    )(own, other, master, moment1, moment2, selector)
    state = pl.pallas_call(
        adam_body,
        out_shape=[jax.ShapeDtypeStruct((rows, columns), jnp.float32)] * 3,
        in_specs=[vmem] * 5,
        out_specs=[pl.BlockSpec(memory_space=pl.ANY)] * 3,
        scratch_shapes=[pltpu.VMEM((rows, columns), jnp.float32)] * 3
        + [pltpu.SemaphoreType.DMA((3, 4))],
        compiler_params=params,
        cost_estimate=pl.CostEstimate(
            flops=20 * size, bytes_accessed=26 * size, transcendentals=0
        ),
    )(own, other, master, moment1, moment2)
    return outgoing, state


def after(value, *earlier):
    return lax.optimization_barrier((value, *earlier))[0]


def combine_body(plan, *refs):
    outs = refs[len(refs) - len(plan) :]
    for out, segments in zip(outs, plan):
        begin = 0
        for rows, terms in segments:
            chunk = next(size for size in (768, 512, rows) if rows % size == 0)

            def one(step, carry, begin=begin, terms=terms, chunk=chunk, out=out):
                total = 0.0
                for source, start in terms:
                    at = pl.multiple_of(start + step * chunk, 16)
                    total = total + refs[source][pl.ds(at, chunk)].astype(jnp.float32)
                at = pl.multiple_of(begin + step * chunk, 16)
                out[pl.ds(at, chunk)] = total.astype(jnp.bfloat16)
                return carry

            lax.fori_loop(0, rows // chunk, one, 0)
            begin += rows


def combine(inputs, plan, flops=0):
    vmem = pl.BlockSpec(memory_space=pltpu.VMEM)
    sizes = [sum(rows for rows, _ in segments) for segments in plan]
    return pl.pallas_call(
        functools.partial(combine_body, plan),
        out_shape=[pltpu.VMEM((size, 128), jnp.bfloat16) for size in sizes],
        in_specs=[vmem] * len(inputs),
        out_specs=[vmem] * len(plan),
        compiler_params=pltpu.CompilerParams(
            vmem_limit_bytes=256 * (sum(sizes) + sum(value.shape[0] for value in inputs)) + 2**21
        ),
        cost_estimate=pl.CostEstimate(flops=flops, bytes_accessed=0, transcendentals=0),
    )(*inputs)


def total(inputs):
    rows = inputs[0].shape[0]
    return combine(inputs, [[(rows, [(k, 0) for k in range(len(inputs))])]])[0]


def summed(tokens, cotangent, early):
    columns = cotangent.shape[1]
    far = (2, 1, 3)
    other = split_sums(tokens, cotangent, [(1, 0, True), (1, 1, True)])
    own = split_sums(tokens, after(cotangent, *other), [(0, 0, True), (0, 1, True)])
    beside = [send(value, rep_pairs(1)) for value in other]
    last = []
    came = []
    for odd in range(2):
        last = [total([own[odd], after(beside[odd], *last)])]
        came.append(send(last[0], swap_pairs(odd)))

    both = split_sums(
        tokens, after(cotangent, *last), [(side, half, False) for side in (1, 0) for half in range(2)]
    )
    beside = [send(value, rep_pairs(1)) for value in both[:4]]

    rows = 8 * columns
    half_sums = combine(
        [both[5], both[7], *came],
        [[(rows, [(odd, 0), (2 + odd, rows)])] for odd in range(2)],
        flops=10**11,
    )
    sent = combine(
        [*half_sums, beside[1], beside[3]],
        [[(rows, [(odd, 0), (2 + odd, 0)])] for odd in range(2)],
    )
    got = [send(sent[odd], swap_pairs(1 - odd)) for odd in range(2)]
    near = combine(
        [both[4], both[6], after(beside[0], *sent), beside[2], *came],
        [[(rows, [(odd, 0), (2 + odd, 0), (4 + odd, 0)])] for odd in range(2)],
    )

    rows = 4 * columns
    sums = [None] * SIDE
    for odd in range(2):
        sums[odd], sums[odd + 2] = combine(
            [near[odd], after(got[odd], early)], [[(rows, [(0, at), (1, at)])] for at in (0, rows)]
        )
    parts = [sums[0]] + [send(sums[at], ring_pairs(1, at)) for at in far]
    sums = combine(
        parts, [[(columns, [(k, at * columns) for k in range(SIDE)])] for at in range(SIDE)]
    )
    return total([sums[0]] + [send(sums[at], ring_pairs(2, at)) for at in (1, 3, 2)])


def select_body(capacity, fsdp_count, owner, selector):
    blocks = owner.shape[1]
    shape = (blocks, blocks)
    mine = owner[pl.ds(lax.axis_index("fsdp"), 1), :]
    by_lane = jnp.broadcast_to(mine, shape)
    earlier = lax.broadcasted_iota(jnp.int32, shape, 0) < lax.broadcasted_iota(jnp.int32, shape, 1)
    same = jnp.where(by_lane.T == by_lane, 1.0, 0.0)
    rank = jnp.sum(jnp.where(earlier, same, 0.0), axis=0, keepdims=True)
    slot = (mine % fsdp_count * capacity).astype(jnp.float32) + rank
    slot = jnp.where(mine // fsdp_count == lax.axis_index("rep"), slot, -1.0)
    rows = blocks * BLOCK_ROWS
    block = lax.broadcasted_iota(jnp.int32, (blocks, rows), 0)
    row = lax.broadcasted_iota(jnp.int32, (blocks, rows), 1)
    spread = jnp.where(row // BLOCK_ROWS == block, 1.0, 0.0).astype(jnp.bfloat16)
    slot = jnp.dot(
        jnp.broadcast_to(slot, (16, blocks)).astype(jnp.bfloat16),
        spread,
        preferred_element_type=jnp.float32,
    )[:1]
    shape = selector.shape
    slot_row = lax.broadcasted_iota(jnp.int32, shape, 0)
    row = lax.broadcasted_iota(jnp.int32, shape, 1)
    at_slot = (slot_row // BLOCK_ROWS).astype(jnp.float32) == slot
    at_row = slot_row % BLOCK_ROWS == row % BLOCK_ROWS
    selector[...] = jnp.where(jnp.logical_and(at_slot, at_row), 1.0, 0.0).astype(jnp.bfloat16)


def select_blocks(owner, capacity, fsdp_count):
    vmem = pl.BlockSpec(memory_space=pltpu.VMEM)
    shape = (fsdp_count * capacity * BLOCK_ROWS, owner.shape[1] * BLOCK_ROWS)
    return pl.pallas_call(
        functools.partial(select_body, capacity, fsdp_count),
        out_shape=jax.ShapeDtypeStruct(shape, jnp.bfloat16),
        in_specs=[vmem],
        out_specs=vmem,
        compiler_params=pltpu.CompilerParams(vmem_limit_bytes=8 * 1024 * 1024),
        cost_estimate=pl.CostEstimate(flops=0, bytes_accessed=0, transcendentals=0),
    )(owner)


def per_device(tokens, cotangent, master, moment1, moment2, owner):
    fsdp_count = lax.axis_size("fsdp")
    rep_count = lax.axis_size("rep")
    shard_rows = master.shape[0]
    columns = master.shape[1]
    local_blocks = shard_rows // BLOCK_ROWS
    capacity = 2 * local_blocks // (rep_count * fsdp_count)
    owner, cotangent = lax.optimization_barrier(
        (owner.reshape(fsdp_count, local_blocks), cotangent)
    )
    selector = select_blocks(owner, capacity, fsdp_count)
    mine = summed(tokens, cotangent, selector)
    beside = send(mine, rep_pairs(2))
    own = jnp.stack([mine, beside])
    other = send(own, rep_pairs(1))
    outgoing, state = adam(own, other, master, moment1, moment2, selector)
    outgoing = outgoing.reshape(fsdp_count, capacity * BLOCK_ROWS, columns)
    received = lax.all_to_all(outgoing, "fsdp", split_axis=0, concat_axis=0, tiled=True)
    upload = unpacked(received.reshape(fsdp_count * capacity * BLOCK_ROWS, columns), BLOCK_ROWS)
    return (*state, upload)


def solution(mesh):
    placed = (
        P(("rep", "fsdp"), None),
        P(("rep", "fsdp"), None),
        P("fsdp", None),
        P("fsdp", None),
        P("fsdp", None),
        P(),
    )
    return jax.shard_map(
        per_device,
        mesh=mesh,
        in_specs=placed,
        out_specs=(
            P("fsdp", None),
            P("fsdp", None),
            P("fsdp", None),
            P(("rep", "fsdp"), None, None),
        ),
        check_vma=False,
    )
```

```python
import functools

import jax
import jax.numpy as jnp
from jax import lax
from jax.experimental import pallas as pl
from jax.experimental.pallas import tpu as pltpu
from jax.sharding import PartitionSpec as P

BLOCK_ROWS = 2
AXES = ("rep", "fsdp")
SIDE = 4

bias_first = 1.0 - 0.9**10
bias_second = 1.0 - 0.95**10

ORDERS = ((0, 1, 2), (1, 2, 0))


def coords(index):
    rep, fsdp = divmod(index, 32)
    y_lo, core = divmod(rep, 2)
    x, rest = divmod(fsdp, 8)
    y_hi, z = divmod(rest, 4)
    return x, y_hi * 2 + y_lo, z, core


def index_of(x, y, z, core):
    return ((y % 2) * 2 + core) * 32 + x * 8 + (y // 2) * 4 + z


def ring_pairs(stage, distance):
    pairs = []
    for device in range(128):
        place = list(coords(device))
        axis = ORDERS[place[3]][stage]
        place[axis] = (place[axis] + distance) % SIDE
        pairs.append((device, index_of(*place)))
    return pairs


def swap_pairs(odd):
    pairs = []
    for device in range(128):
        place = list(coords(device))
        axis = ORDERS[place[3]][0]
        place[axis] = (((place[axis] + odd) ^ 1) - odd) % SIDE
        pairs.append((device, index_of(*place)))
    return pairs


def rep_pairs(bit):
    return [(device, (((device // 32) ^ bit) * 32) + device % 32) for device in range(128)]


def send(value, pairs):
    return lax.ppermute(value, AXES, pairs)


def split_body(groups, cot, tokens, *refs):
    outs, (cot_t, held, kept, in_sem, cot_sem, sem) = refs[:-6], refs[-6:]
    columns = cot.shape[1]
    count = SIDE * SIDE
    rep, fsdp = lax.axis_index("rep"), lax.axis_index("fsdp")
    core, y_lo = lax.rem(rep, 2), rep // 2
    place = (fsdp // 8, lax.rem(fsdp // 4, 2) * 2 + y_lo, lax.rem(fsdp, 4))

    def fetch(at):
        side, half, is_sent = groups[at]
        target = core if side == 0 else 1 - core
        is_first = target == 0
        parity = lax.rem(jnp.where(is_first, place[0], place[1]), 2)
        even, odd = 1 + 2 * parity, 3 - 2 * parity
        distances = (odd if half else even, 2) if is_sent else (0, even if half else odd)
        tile = 0
        for one in distances:
            for two in (1 - half, 3 - half):
                for three in range(SIDE):
                    x = lax.rem(place[0] + jnp.where(is_first, one, three), SIDE)
                    y = lax.rem(place[1] + jnp.where(is_first, two, one), SIDE)
                    z = lax.rem(place[2] + jnp.where(is_first, three, two), SIDE)
                    lane = (x * 8 + (y // 2) * 4 + z) * 512 + lax.rem(y, 2) * 256 + target * 128
                    pltpu.make_async_copy(
                        tokens.at[:, pl.ds(pl.multiple_of(lane, 128), 128)],
                        held.at[at, :, pl.ds(tile * 128, 128)],
                        in_sem.at[at],
                    ).start()
                    tile += 1

    cot_copy = pltpu.make_async_copy(cot, cot_t.at[1], cot_sem)
    cot_copy.start()
    fetch(0)
    fetch(1)
    cot_copy.wait()
    cot_t[0] = cot_t[1].T
    copies = []
    done = 0
    for at in range(len(groups)):
        pltpu.make_async_copy(held.at[at], held.at[at], in_sem.at[at]).wait()
        if at + 2 < len(groups):
            fetch(at + 2)
        total = jnp.dot(cot_t[0], held[at], preferred_element_type=jnp.float32)
        parts = 1 if groups[at][2] else 2
        per_part = count // parts
        rows = per_part * columns
        for tile in range(count):
            piece = total[:, tile * 128 : (tile + 1) * 128].astype(jnp.bfloat16)
            part, index = divmod(tile, per_part)
            if groups[at][0] == 0:
                outs[done + part][index * columns : (index + 1) * columns] = piece
            else:
                kept[at, tile * columns : (tile + 1) * columns] = piece
        for part in range(parts):
            if groups[at][0] == 1:
                copy = pltpu.make_async_copy(
                    kept.at[at, pl.ds(part * rows, rows)], outs[done], sem.at[done]
                )
                copy.start()
                copies.append(copy)
            done += 1
    for copy in copies:
        copy.wait()


def split_sums(tokens, cotangent, groups):
    depth = tokens.shape[0]
    columns = cotangent.shape[1]
    rows = SIDE * SIDE * columns
    outs, specs = [], []
    for side, _, is_sent in groups:
        sizes = [rows] if is_sent else [rows // 2] * 2
        for size in sizes:
            place = pltpu.HBM if side else pltpu.VMEM
            outs.append(place((size, 128), jnp.bfloat16))
            specs.append(pl.BlockSpec(memory_space=pl.ANY if side else pltpu.VMEM))
    leaving = max(1, sum(side for side, _, _ in groups))
    return pl.pallas_call(
        functools.partial(split_body, groups),
        out_shape=outs,
        in_specs=[pl.BlockSpec(memory_space=pl.ANY)] * 2,
        out_specs=specs,
        scratch_shapes=[
            pltpu.VMEM((2, columns, depth), jnp.bfloat16),
            pltpu.VMEM((len(groups), depth, SIDE * SIDE * 128), jnp.bfloat16),
            pltpu.VMEM((leaving, rows, 128), jnp.bfloat16),
            pltpu.SemaphoreType.DMA((len(groups),)),
            pltpu.SemaphoreType.DMA,
            pltpu.SemaphoreType.DMA((len(outs),)),
        ],
        compiler_params=pltpu.CompilerParams(vmem_limit_bytes=32 * 1024 * 1024),
        cost_estimate=pl.CostEstimate(
            flops=2 * depth * rows * 128 * len(groups),
            bytes_accessed=512 * rows * len(groups),
            transcendentals=0,
        ),
    )(
        pltpu.with_memory_space_constraint(cotangent, pltpu.HBM),
        pltpu.with_memory_space_constraint(tokens, pltpu.HBM),
    )


def updated(grad, master, moment1, moment2):
    first = 0.9 * moment1 + 0.1 * grad
    second = 0.95 * moment2 + 0.05 * grad * grad
    update = first / bias_first / (jnp.sqrt(second / bias_second) + 1e-08)
    return master - 0.05 * (update + 0.1 * master), first, second


def rep_grad(own, other, at):
    rep = lax.axis_index("rep")
    core, y_lo = lax.rem(rep, 2), rep // 2
    index = y_lo if at // 2 == 0 else 1 - y_lo
    piece = jnp.where(core == at % 2, own[index], other[index])
    return piece.T.astype(jnp.float32)


def adam_body(own, other, master, moment1, moment2, selector, *refs):
    outgoing, outs, weight, kept, sem = refs[0], refs[1:4], refs[4], refs[5:8], refs[8]
    copies = []
    for at in range(4):
        rows = slice(at * 128, (at + 1) * 128)
        values = updated(rep_grad(own, other, at), master[rows], moment1[rows], moment2[rows])
        weight[rows] = values[0].astype(jnp.bfloat16)
        for k in range(3):
            kept[k][rows] = values[k]
            copy = pltpu.make_async_copy(
                kept[k].at[pl.ds(at * 128, 128)], outs[k].at[pl.ds(at * 128, 128)], sem.at[k, at]
            )
            copy.start()
            copies.append(copy)
    chosen = jnp.dot(selector[...], weight[...], preferred_element_type=jnp.float32)
    outgoing[...] = chosen.astype(jnp.bfloat16).reshape(outgoing.shape)
    for copy in copies:
        copy.wait()


def adam(own, other, master, moment1, moment2, selector):
    rows, columns = master.shape
    size = rows * columns
    vmem = pl.BlockSpec(memory_space=pltpu.VMEM)
    slots = (selector.shape[0] // BLOCK_ROWS, BLOCK_ROWS, columns)
    outgoing, *state = pl.pallas_call(
        adam_body,
        out_shape=[jax.ShapeDtypeStruct(slots, jnp.bfloat16)]
        + [jax.ShapeDtypeStruct((rows, columns), jnp.float32)] * 3,
        in_specs=[vmem] * 6,
        out_specs=[vmem] + [pl.BlockSpec(memory_space=pl.ANY)] * 3,
        scratch_shapes=[pltpu.VMEM((rows, columns), jnp.bfloat16)]
        + [pltpu.VMEM((rows, columns), jnp.float32)] * 3
        + [pltpu.SemaphoreType.DMA((3, 4))],
        compiler_params=pltpu.CompilerParams(vmem_limit_bytes=16 * 1024 * 1024),
        cost_estimate=pl.CostEstimate(
            flops=20 * size, bytes_accessed=26 * size, transcendentals=0
        ),
    )(own, other, master, moment1, moment2, selector)
    return outgoing, state


def after(value, *earlier):
    return lax.optimization_barrier((value, *earlier))[0]


def combine_body(plan, *refs):
    outs = refs[len(refs) - len(plan) :]
    for out, segments in zip(outs, plan):
        begin = 0
        for rows, terms in segments:
            chunk = next(size for size in (768, 512, rows) if rows % size == 0)

            def one(step, carry, begin=begin, terms=terms, chunk=chunk, out=out):
                total = 0.0
                for source, start in terms:
                    at = pl.multiple_of(start + step * chunk, 16)
                    total = total + refs[source][pl.ds(at, chunk)].astype(jnp.float32)
                at = pl.multiple_of(begin + step * chunk, 16)
                out[pl.ds(at, chunk)] = total.astype(jnp.bfloat16)
                return carry

            lax.fori_loop(0, rows // chunk, one, 0)
            begin += rows


def combine(inputs, plan, flops=0):
    vmem = pl.BlockSpec(memory_space=pltpu.VMEM)
    sizes = [sum(rows for rows, _ in segments) for segments in plan]
    return pl.pallas_call(
        functools.partial(combine_body, plan),
        out_shape=[pltpu.VMEM((size, 128), jnp.bfloat16) for size in sizes],
        in_specs=[vmem] * len(inputs),
        out_specs=[vmem] * len(plan),
        compiler_params=pltpu.CompilerParams(
            vmem_limit_bytes=256 * (sum(sizes) + sum(value.shape[0] for value in inputs)) + 2**21
        ),
        cost_estimate=pl.CostEstimate(flops=flops, bytes_accessed=0, transcendentals=0),
    )(*inputs)


def total(inputs):
    rows = inputs[0].shape[0]
    return combine(inputs, [[(rows, [(k, 0) for k in range(len(inputs))])]])[0]


def summed(tokens, cotangent, early):
    columns = cotangent.shape[1]
    far = (2, 1, 3)
    other = split_sums(tokens, cotangent, [(1, 0, True), (1, 1, True)])
    own = split_sums(tokens, after(cotangent, *other), [(0, 0, True), (0, 1, True)])
    beside = [send(value, rep_pairs(1)) for value in other]
    last = []
    came = []
    for odd in range(2):
        last = [total([own[odd], after(beside[odd], *last)])]
        came.append(send(last[0], swap_pairs(odd)))

    both = split_sums(
        tokens, after(cotangent, *last), [(side, half, False) for side in (1, 0) for half in range(2)]
    )
    beside = [send(value, rep_pairs(1)) for value in both[:4]]

    rows = 8 * columns
    half_sums = combine(
        [both[5], both[7], *came],
        [[(rows, [(odd, 0), (2 + odd, rows)])] for odd in range(2)],
        flops=10**11,
    )
    sent = combine(
        [*half_sums, beside[1], beside[3]],
        [[(rows, [(odd, 0), (2 + odd, 0)])] for odd in range(2)],
    )
    got = [send(sent[odd], swap_pairs(1 - odd)) for odd in range(2)]
    near = combine(
        [both[4], both[6], after(beside[0], *sent), beside[2], *came],
        [[(rows, [(odd, 0), (2 + odd, 0), (4 + odd, 0)])] for odd in range(2)],
    )

    rows = 4 * columns
    sums = [None] * SIDE
    for odd in range(2):
        sums[1 - odd], sums[3 - odd] = combine(
            [near[odd], after(got[odd], early)], [[(rows, [(0, at), (1, at)])] for at in (0, rows)]
        )
    parts = [sums[0]] + [send(sums[at], ring_pairs(1, at)) for at in far]
    sums = combine(
        parts, [[(columns, [(k, at * columns) for k in range(SIDE)])] for at in range(SIDE)]
    )
    return total([sums[0]] + [send(sums[at], ring_pairs(2, at)) for at in (1, 3, 2)])


def select_body(capacity, fsdp_count, owner, selector):
    blocks = owner.shape[0] // fsdp_count
    shape = (blocks, blocks)
    first = pl.multiple_of(lax.axis_index("fsdp") * blocks, blocks)
    mine = owner[pl.ds(first, blocks)].reshape(1, blocks)
    by_lane = jnp.broadcast_to(mine, shape)
    earlier = lax.broadcasted_iota(jnp.int32, shape, 0) < lax.broadcasted_iota(jnp.int32, shape, 1)
    same = jnp.where(by_lane.T == by_lane, 1.0, 0.0)
    rank = jnp.sum(jnp.where(earlier, same, 0.0), axis=0, keepdims=True)
    slot = (mine % fsdp_count * capacity).astype(jnp.float32) + rank
    slot = jnp.where(mine // fsdp_count == lax.axis_index("rep"), slot, -1.0)
    rows = blocks * BLOCK_ROWS
    block = lax.broadcasted_iota(jnp.int32, (blocks, rows), 0)
    row = lax.broadcasted_iota(jnp.int32, (blocks, rows), 1)
    spread = jnp.where(row // BLOCK_ROWS == block, 1.0, 0.0).astype(jnp.bfloat16)
    slot = jnp.dot(
        jnp.broadcast_to(slot, (16, blocks)).astype(jnp.bfloat16),
        spread,
        preferred_element_type=jnp.float32,
    )[:1]
    shape = selector.shape
    slot_row = lax.broadcasted_iota(jnp.int32, shape, 0)
    row = lax.broadcasted_iota(jnp.int32, shape, 1)
    at_slot = (slot_row // BLOCK_ROWS).astype(jnp.float32) == slot
    at_row = slot_row % BLOCK_ROWS == row % BLOCK_ROWS
    selector[...] = jnp.where(jnp.logical_and(at_slot, at_row), 1.0, 0.0).astype(jnp.bfloat16)


def select_blocks(owner, capacity, fsdp_count):
    vmem = pl.BlockSpec(memory_space=pltpu.VMEM)
    shape = (fsdp_count * capacity * BLOCK_ROWS, owner.shape[0] // fsdp_count * BLOCK_ROWS)
    return pl.pallas_call(
        functools.partial(select_body, capacity, fsdp_count),
        out_shape=jax.ShapeDtypeStruct(shape, jnp.bfloat16),
        in_specs=[vmem],
        out_specs=vmem,
        compiler_params=pltpu.CompilerParams(vmem_limit_bytes=8 * 1024 * 1024),
        cost_estimate=pl.CostEstimate(flops=0, bytes_accessed=0, transcendentals=0),
    )(owner)


def per_device(tokens, cotangent, master, moment1, moment2, owner):
    fsdp_count = lax.axis_size("fsdp")
    rep_count = lax.axis_size("rep")
    shard_rows = master.shape[0]
    columns = master.shape[1]
    local_blocks = shard_rows // BLOCK_ROWS
    capacity = 2 * local_blocks // (rep_count * fsdp_count)
    selector = select_blocks(owner, capacity, fsdp_count)
    mine = summed(tokens, cotangent, selector)
    beside = send(mine, rep_pairs(2))
    own = jnp.stack([mine, beside])
    other = send(own, rep_pairs(1))
    outgoing, state = adam(own, other, master, moment1, moment2, selector)
    outgoing = outgoing.reshape(fsdp_count, capacity, BLOCK_ROWS, columns)
    received = lax.all_to_all(outgoing, "fsdp", split_axis=0, concat_axis=0, tiled=True)
    upload = received.reshape(fsdp_count * capacity, BLOCK_ROWS, columns)
    return (*state, upload)


def solution(mesh):
    placed = (
        P(("rep", "fsdp"), None),
        P(("rep", "fsdp"), None),
        P("fsdp", None),
        P("fsdp", None),
        P("fsdp", None),
        P(),
    )
    return jax.shard_map(
        per_device,
        mesh=mesh,
        in_specs=placed,
        out_specs=(
            P("fsdp", None),
            P("fsdp", None),
            P("fsdp", None),
            P(("rep", "fsdp"), None, None),
        ),
        check_vma=False,
    )
```

```python
import functools

import jax
import jax.numpy as jnp
from jax import lax
from jax.experimental import pallas as pl
from jax.experimental.pallas import tpu as pltpu
from jax.sharding import PartitionSpec as P

BLOCK_ROWS = 2
AXES = ("rep", "fsdp")
SIDE = 4

bias_first = 1.0 - 0.9**10
bias_second = 1.0 - 0.95**10

ORDERS = ((0, 1, 2), (1, 2, 0))


def coords(index):
    rep, fsdp = divmod(index, 32)
    y_lo, core = divmod(rep, 2)
    x, rest = divmod(fsdp, 8)
    y_hi, z = divmod(rest, 4)
    return x, y_hi * 2 + y_lo, z, core


def index_of(x, y, z, core):
    return ((y % 2) * 2 + core) * 32 + x * 8 + (y // 2) * 4 + z


def far_pairs(stage):
    pairs = []
    for device in range(128):
        place = list(coords(device))
        axis = ORDERS[place[3]][stage]
        place[axis] = (place[axis] + 2) % SIDE
        pairs.append((device, index_of(*place)))
    return pairs


def swap_pairs(odd, stage=0):
    pairs = []
    for device in range(128):
        place = list(coords(device))
        axis = ORDERS[place[3]][stage]
        place[axis] = (((place[axis] + odd) ^ 1) - odd) % SIDE
        pairs.append((device, index_of(*place)))
    return pairs


def rep_pairs(bit):
    return [(device, (((device // 32) ^ bit) * 32) + device % 32) for device in range(128)]


def send(value, pairs):
    return lax.ppermute(value, AXES, pairs)


def split_body(groups, cot, tokens, *refs):
    outs, (cot_t, held, kept, in_sem, cot_sem, sem) = refs[:-6], refs[-6:]
    columns = cot.shape[1]
    count = SIDE * SIDE
    rep, fsdp = lax.axis_index("rep"), lax.axis_index("fsdp")
    core, y_lo = lax.rem(rep, 2), rep // 2
    place = (fsdp // 8, lax.rem(fsdp // 4, 2) * 2 + y_lo, lax.rem(fsdp, 4))

    def fetch(at):
        side, half, is_sent = groups[at]
        target = core if side == 0 else 1 - core
        is_first = target == 0
        near = []
        for axis in range(3):
            along = jnp.where(is_first, place[ORDERS[0][axis]], place[ORDERS[1][axis]])
            parity = lax.rem(along, 2)
            near.append((1 + 2 * parity, 3 - 2 * parity))
        if is_sent:
            distances = (near[0][half], 2)
        else:
            distances = (0, near[0][1 - half])
        tile = 0
        for one in distances:
            for two in near[1] if half else (0, 2):
                for three in (0, 2, *near[2]):
                    x = lax.rem(place[0] + jnp.where(is_first, one, three), SIDE)
                    y = lax.rem(place[1] + jnp.where(is_first, two, one), SIDE)
                    z = lax.rem(place[2] + jnp.where(is_first, three, two), SIDE)
                    lane = (x * 8 + (y // 2) * 4 + z) * 512 + lax.rem(y, 2) * 256 + target * 128
                    pltpu.make_async_copy(
                        tokens.at[:, pl.ds(pl.multiple_of(lane, 128), 128)],
                        held.at[at, :, pl.ds(tile * 128, 128)],
                        in_sem.at[at],
                    ).start()
                    tile += 1

    cot_copy = pltpu.make_async_copy(cot, cot_t.at[1], cot_sem)
    cot_copy.start()
    fetch(0)
    fetch(1)
    cot_copy.wait()
    cot_t[0] = cot_t[1].T
    copies = []
    done = 0
    for at in range(len(groups)):
        pltpu.make_async_copy(held.at[at], held.at[at], in_sem.at[at]).wait()
        if at + 2 < len(groups):
            fetch(at + 2)
        total = jnp.dot(cot_t[0], held[at], preferred_element_type=jnp.float32)
        parts = 1 if groups[at][2] else 2
        per_part = count // parts
        rows = per_part * columns
        for tile in range(count):
            piece = total[:, tile * 128 : (tile + 1) * 128].astype(jnp.bfloat16)
            part, index = divmod(tile, per_part)
            if groups[at][0] == 0:
                outs[done + part][index * columns : (index + 1) * columns] = piece
            else:
                kept[at, tile * columns : (tile + 1) * columns] = piece
        for part in range(parts):
            if groups[at][0] == 1:
                copy = pltpu.make_async_copy(
                    kept.at[at, pl.ds(part * rows, rows)], outs[done], sem.at[done]
                )
                copy.start()
                copies.append(copy)
            done += 1
    for copy in copies:
        copy.wait()


def split_sums(tokens, cotangent, groups):
    depth = tokens.shape[0]
    columns = cotangent.shape[1]
    rows = SIDE * SIDE * columns
    outs, specs = [], []
    for side, _, is_sent in groups:
        sizes = [rows] if is_sent else [rows // 2] * 2
        for size in sizes:
            place = pltpu.HBM if side else pltpu.VMEM
            outs.append(place((size, 128), jnp.bfloat16))
            specs.append(pl.BlockSpec(memory_space=pl.ANY if side else pltpu.VMEM))
    leaving = max(1, sum(side for side, _, _ in groups))
    return pl.pallas_call(
        functools.partial(split_body, groups),
        out_shape=outs,
        in_specs=[pl.BlockSpec(memory_space=pl.ANY)] * 2,
        out_specs=specs,
        scratch_shapes=[
            pltpu.VMEM((2, columns, depth), jnp.bfloat16),
            pltpu.VMEM((len(groups), depth, SIDE * SIDE * 128), jnp.bfloat16),
            pltpu.VMEM((leaving, rows, 128), jnp.bfloat16),
            pltpu.SemaphoreType.DMA((len(groups),)),
            pltpu.SemaphoreType.DMA,
            pltpu.SemaphoreType.DMA((len(outs),)),
        ],
        compiler_params=pltpu.CompilerParams(vmem_limit_bytes=32 * 1024 * 1024),
        cost_estimate=pl.CostEstimate(
            flops=2 * depth * rows * 128 * len(groups),
            bytes_accessed=512 * rows * len(groups),
            transcendentals=0,
        ),
    )(
        pltpu.with_memory_space_constraint(cotangent, pltpu.HBM),
        pltpu.with_memory_space_constraint(tokens, pltpu.HBM),
    )


def updated(grad, master, moment1, moment2):
    first = 0.9 * moment1 + 0.1 * grad
    second = 0.95 * moment2 + 0.05 * grad * grad
    update = first / bias_first / (jnp.sqrt(second / bias_second) + 1e-08)
    return master - 0.05 * (update + 0.1 * master), first, second


def rep_grad(own, other, at):
    rep = lax.axis_index("rep")
    core, y_lo = lax.rem(rep, 2), rep // 2
    index = y_lo if at // 2 == 0 else 1 - y_lo
    piece = jnp.where(core == at % 2, own[index], other[index])
    return piece.T.astype(jnp.float32)


def adam_body(own, other, master, moment1, moment2, selector, *refs):
    outgoing, outs, weight, kept, sem = refs[0], refs[1:4], refs[4], refs[5:8], refs[8]
    copies = []
    for at in range(4):
        rows = slice(at * 128, (at + 1) * 128)
        values = updated(rep_grad(own, other, at), master[rows], moment1[rows], moment2[rows])
        weight[rows] = values[0].astype(jnp.bfloat16)
        for k in range(3):
            kept[k][rows] = values[k]
            copy = pltpu.make_async_copy(
                kept[k].at[pl.ds(at * 128, 128)], outs[k].at[pl.ds(at * 128, 128)], sem.at[k, at]
            )
            copy.start()
            copies.append(copy)
    chosen = jnp.dot(selector[...], weight[...], preferred_element_type=jnp.float32)
    outgoing[...] = chosen.astype(jnp.bfloat16).reshape(outgoing.shape)
    for copy in copies:
        copy.wait()


def adam(own, other, master, moment1, moment2, selector):
    rows, columns = master.shape
    size = rows * columns
    vmem = pl.BlockSpec(memory_space=pltpu.VMEM)
    slots = (selector.shape[0] // BLOCK_ROWS, BLOCK_ROWS, columns)
    outgoing, *state = pl.pallas_call(
        adam_body,
        out_shape=[jax.ShapeDtypeStruct(slots, jnp.bfloat16)]
        + [jax.ShapeDtypeStruct((rows, columns), jnp.float32)] * 3,
        in_specs=[vmem] * 6,
        out_specs=[vmem] + [pl.BlockSpec(memory_space=pl.ANY)] * 3,
        scratch_shapes=[pltpu.VMEM((rows, columns), jnp.bfloat16)]
        + [pltpu.VMEM((rows, columns), jnp.float32)] * 3
        + [pltpu.SemaphoreType.DMA((3, 4))],
        compiler_params=pltpu.CompilerParams(vmem_limit_bytes=16 * 1024 * 1024),
        cost_estimate=pl.CostEstimate(
            flops=20 * size, bytes_accessed=26 * size, transcendentals=0
        ),
    )(own, other, master, moment1, moment2, selector)
    return outgoing, state


def after(value, *earlier):
    return lax.optimization_barrier((value, *earlier))[0]


def combine_body(plan, *refs):
    outs = refs[len(refs) - len(plan) :]
    for out, segments in zip(outs, plan):
        begin = 0
        for rows, terms in segments:
            chunk = next(size for size in (768, 512, rows) if rows % size == 0)

            def one(step, carry, begin=begin, terms=terms, chunk=chunk, out=out):
                total = 0.0
                for source, start in terms:
                    at = pl.multiple_of(start + step * chunk, 16)
                    total = total + refs[source][pl.ds(at, chunk)].astype(jnp.float32)
                at = pl.multiple_of(begin + step * chunk, 16)
                out[pl.ds(at, chunk)] = total.astype(jnp.bfloat16)
                return carry

            lax.fori_loop(0, rows // chunk, one, 0)
            begin += rows


def combine(inputs, plan, flops=0):
    vmem = pl.BlockSpec(memory_space=pltpu.VMEM)
    sizes = [sum(rows for rows, _ in segments) for segments in plan]
    return pl.pallas_call(
        functools.partial(combine_body, plan),
        out_shape=[pltpu.VMEM((size, 128), jnp.bfloat16) for size in sizes],
        in_specs=[vmem] * len(inputs),
        out_specs=[vmem] * len(plan),
        compiler_params=pltpu.CompilerParams(
            vmem_limit_bytes=256 * (sum(sizes) + sum(value.shape[0] for value in inputs)) + 2**21
        ),
        cost_estimate=pl.CostEstimate(flops=flops, bytes_accessed=0, transcendentals=0),
    )(*inputs)


def total(inputs):
    rows = inputs[0].shape[0]
    return combine(inputs, [[(rows, [(k, 0) for k in range(len(inputs))])]])[0]


def exchanged(sums, stage):
    stay, far, even, odd = sums
    return [
        stay,
        send(even, swap_pairs(0, stage)),
        send(odd, swap_pairs(1, stage)),
        send(far, far_pairs(stage)),
    ]


def summed(tokens, cotangent, early):
    columns = cotangent.shape[1]
    other = split_sums(tokens, cotangent, [(1, 0, True), (1, 1, True)])
    own = split_sums(tokens, after(cotangent, *other), [(0, 0, True), (0, 1, True)])
    beside = [send(value, rep_pairs(1)) for value in other]
    last = []
    came = []
    for odd in range(2):
        last = [total([own[odd], after(beside[odd], *last)])]
        came.append(send(last[0], swap_pairs(odd)))

    both = split_sums(
        tokens, after(cotangent, *last), [(side, half, False) for side in (1, 0) for half in range(2)]
    )
    beside = [send(value, rep_pairs(1)) for value in both[:4]]

    rows = 8 * columns
    half_sums = combine(
        [both[5], both[7], *came],
        [[(rows, [(odd, 0), (2 + odd, rows)])] for odd in range(2)],
        flops=10**11,
    )
    sent = combine(
        [*half_sums, beside[1], beside[3]],
        [[(rows, [(odd, 0), (2 + odd, 0)])] for odd in range(2)],
    )
    got = [send(sent[odd], swap_pairs(1 - odd)) for odd in range(2)]
    near = combine(
        [both[4], both[6], after(beside[0], *sent), beside[2], *came],
        [[(rows, [(odd, 0), (2 + odd, 0), (4 + odd, 0)])] for odd in range(2)],
    )

    rows = 4 * columns
    sums = []
    for odd in range(2):
        sums += combine(
            [near[odd], after(got[odd], early)], [[(rows, [(0, at), (1, at)])] for at in (0, rows)]
        )
    sums = combine(
        exchanged(sums, 1),
        [[(columns, [(k, at * columns) for k in range(SIDE)])] for at in range(SIDE)],
    )
    return total(exchanged(sums, 2))


def select_body(capacity, fsdp_count, owner, selector):
    blocks = owner.shape[0] // fsdp_count
    shape = (blocks, blocks)
    first = pl.multiple_of(lax.axis_index("fsdp") * blocks, blocks)
    mine = owner[pl.ds(first, blocks)].reshape(1, blocks)
    by_lane = jnp.broadcast_to(mine, shape)
    earlier = lax.broadcasted_iota(jnp.int32, shape, 0) < lax.broadcasted_iota(jnp.int32, shape, 1)
    same = jnp.where(by_lane.T == by_lane, 1.0, 0.0)
    rank = jnp.sum(jnp.where(earlier, same, 0.0), axis=0, keepdims=True)
    slot = (mine % fsdp_count * capacity).astype(jnp.float32) + rank
    slot = jnp.where(mine // fsdp_count == lax.axis_index("rep"), slot, -1.0)
    rows = blocks * BLOCK_ROWS
    block = lax.broadcasted_iota(jnp.int32, (blocks, rows), 0)
    row = lax.broadcasted_iota(jnp.int32, (blocks, rows), 1)
    spread = jnp.where(row // BLOCK_ROWS == block, 1.0, 0.0).astype(jnp.bfloat16)
    slot = jnp.dot(
        jnp.broadcast_to(slot, (16, blocks)).astype(jnp.bfloat16),
        spread,
        preferred_element_type=jnp.float32,
    )[:1]
    shape = selector.shape
    slot_row = lax.broadcasted_iota(jnp.int32, shape, 0)
    row = lax.broadcasted_iota(jnp.int32, shape, 1)
    at_slot = (slot_row // BLOCK_ROWS).astype(jnp.float32) == slot
    at_row = slot_row % BLOCK_ROWS == row % BLOCK_ROWS
    selector[...] = jnp.where(jnp.logical_and(at_slot, at_row), 1.0, 0.0).astype(jnp.bfloat16)


def select_blocks(owner, capacity, fsdp_count):
    vmem = pl.BlockSpec(memory_space=pltpu.VMEM)
    shape = (fsdp_count * capacity * BLOCK_ROWS, owner.shape[0] // fsdp_count * BLOCK_ROWS)
    return pl.pallas_call(
        functools.partial(select_body, capacity, fsdp_count),
        out_shape=jax.ShapeDtypeStruct(shape, jnp.bfloat16),
        in_specs=[vmem],
        out_specs=vmem,
        compiler_params=pltpu.CompilerParams(vmem_limit_bytes=8 * 1024 * 1024),
        cost_estimate=pl.CostEstimate(flops=0, bytes_accessed=0, transcendentals=0),
    )(owner)


def per_device(tokens, cotangent, master, moment1, moment2, owner):
    fsdp_count = lax.axis_size("fsdp")
    rep_count = lax.axis_size("rep")
    shard_rows = master.shape[0]
    columns = master.shape[1]
    local_blocks = shard_rows // BLOCK_ROWS
    capacity = 2 * local_blocks // (rep_count * fsdp_count)
    selector = select_blocks(owner, capacity, fsdp_count)
    mine = summed(tokens, cotangent, selector)
    beside = send(mine, rep_pairs(2))
    own = jnp.stack([mine, beside])
    other = send(own, rep_pairs(1))
    outgoing, state = adam(own, other, master, moment1, moment2, selector)
    outgoing = outgoing.reshape(fsdp_count, capacity, BLOCK_ROWS, columns)
    received = lax.all_to_all(outgoing, "fsdp", split_axis=0, concat_axis=0, tiled=True)
    upload = received.reshape(fsdp_count * capacity, BLOCK_ROWS, columns)
    return (*state, upload)


def solution(mesh):
    placed = (
        P(("rep", "fsdp"), None),
        P(("rep", "fsdp"), None),
        P("fsdp", None),
        P("fsdp", None),
        P("fsdp", None),
        P(),
    )
    return jax.shard_map(
        per_device,
        mesh=mesh,
        in_specs=placed,
        out_specs=(
            P("fsdp", None),
            P("fsdp", None),
            P("fsdp", None),
            P(("rep", "fsdp"), None, None),
        ),
        check_vma=False,
    )
```

```python
import functools

import jax
import jax.numpy as jnp
from jax import lax
from jax.experimental import pallas as pl
from jax.experimental.pallas import tpu as pltpu
from jax.sharding import PartitionSpec as P

BLOCK_ROWS = 2
AXES = ("rep", "fsdp")
SIDE = 4

bias_first = 1.0 - 0.9**10
bias_second = 1.0 - 0.95**10

ORDERS = ((0, 1, 2), (1, 2, 0))


def coords(index):
    rep, fsdp = divmod(index, 32)
    y_lo, core = divmod(rep, 2)
    x, rest = divmod(fsdp, 8)
    y_hi, z = divmod(rest, 4)
    return x, y_hi * 2 + y_lo, z, core


def index_of(x, y, z, core):
    return ((y % 2) * 2 + core) * 32 + x * 8 + (y // 2) * 4 + z


def far_pairs(stage):
    pairs = []
    for device in range(128):
        place = list(coords(device))
        axis = ORDERS[place[3]][stage]
        place[axis] = (place[axis] + 2) % SIDE
        pairs.append((device, index_of(*place)))
    return pairs


def swap_pairs(odd, stage=0):
    pairs = []
    for device in range(128):
        place = list(coords(device))
        axis = ORDERS[place[3]][stage]
        place[axis] = (((place[axis] + odd) ^ 1) - odd) % SIDE
        pairs.append((device, index_of(*place)))
    return pairs


def rep_pairs(bit):
    return [(device, (((device // 32) ^ bit) * 32) + device % 32) for device in range(128)]


def send(value, pairs):
    return lax.ppermute(value, AXES, pairs)


def split_body(groups, cot, tokens, *refs):
    outs, (cot_t, held, kept, in_sem, cot_sem, sem) = refs[:-6], refs[-6:]
    columns = cot.shape[1]
    count = SIDE * SIDE
    rep, fsdp = lax.axis_index("rep"), lax.axis_index("fsdp")
    core, y_lo = lax.rem(rep, 2), rep // 2
    place = (fsdp // 8, lax.rem(fsdp // 4, 2) * 2 + y_lo, lax.rem(fsdp, 4))

    def fetch(at):
        side, half, is_sent = groups[at]
        target = core if side == 0 else 1 - core
        is_first = target == 0
        near = []
        for axis in range(3):
            along = jnp.where(is_first, place[ORDERS[0][axis]], place[ORDERS[1][axis]])
            parity = lax.rem(along, 2)
            near.append((1 + 2 * parity, 3 - 2 * parity))
        if is_sent:
            distances = (near[0][half], 2)
        else:
            distances = (0, near[0][1 - half])
        tile = 0
        for one in distances:
            for two in near[1] if half else (0, 2):
                for three in (0, 2, *near[2]):
                    x = lax.rem(place[0] + jnp.where(is_first, one, three), SIDE)
                    y = lax.rem(place[1] + jnp.where(is_first, two, one), SIDE)
                    z = lax.rem(place[2] + jnp.where(is_first, three, two), SIDE)
                    lane = (x * 8 + (y // 2) * 4 + z) * 512 + lax.rem(y, 2) * 256 + target * 128
                    pltpu.make_async_copy(
                        tokens.at[:, pl.ds(pl.multiple_of(lane, 128), 128)],
                        held.at[at, :, pl.ds(tile * 128, 128)],
                        in_sem.at[at],
                    ).start()
                    tile += 1

    cot_copy = pltpu.make_async_copy(cot, cot_t.at[1], cot_sem)
    cot_copy.start()
    fetch(0)
    fetch(1)
    cot_copy.wait()
    cot_t[0] = cot_t[1].T
    copies = []
    done = 0
    for at in range(len(groups)):
        pltpu.make_async_copy(held.at[at], held.at[at], in_sem.at[at]).wait()
        if at + 2 < len(groups):
            fetch(at + 2)
        total = jnp.dot(cot_t[0], held[at], preferred_element_type=jnp.float32)
        parts = 1 if groups[at][2] else 2
        per_part = count // parts
        rows = per_part * columns
        for tile in range(count):
            piece = total[:, tile * 128 : (tile + 1) * 128].astype(jnp.bfloat16)
            part, index = divmod(tile, per_part)
            if groups[at][0] == 0:
                outs[done + part][index * columns : (index + 1) * columns] = piece
            else:
                kept[at, tile * columns : (tile + 1) * columns] = piece
        for part in range(parts):
            if groups[at][0] == 1:
                copy = pltpu.make_async_copy(
                    kept.at[at, pl.ds(part * rows, rows)], outs[done], sem.at[done]
                )
                copy.start()
                copies.append(copy)
            done += 1
    for copy in copies:
        copy.wait()


def split_sums(tokens, cotangent, groups):
    depth = tokens.shape[0]
    columns = cotangent.shape[1]
    rows = SIDE * SIDE * columns
    outs, specs = [], []
    for side, _, is_sent in groups:
        sizes = [rows] if is_sent else [rows // 2] * 2
        for size in sizes:
            place = pltpu.HBM if side else pltpu.VMEM
            outs.append(place((size, 128), jnp.bfloat16))
            specs.append(pl.BlockSpec(memory_space=pl.ANY if side else pltpu.VMEM))
    leaving = max(1, sum(side for side, _, _ in groups))
    return pl.pallas_call(
        functools.partial(split_body, groups),
        out_shape=outs,
        in_specs=[pl.BlockSpec(memory_space=pl.ANY)] * 2,
        out_specs=specs,
        scratch_shapes=[
            pltpu.VMEM((2, columns, depth), jnp.bfloat16),
            pltpu.VMEM((len(groups), depth, SIDE * SIDE * 128), jnp.bfloat16),
            pltpu.VMEM((leaving, rows, 128), jnp.bfloat16),
            pltpu.SemaphoreType.DMA((len(groups),)),
            pltpu.SemaphoreType.DMA,
            pltpu.SemaphoreType.DMA((len(outs),)),
        ],
        compiler_params=pltpu.CompilerParams(vmem_limit_bytes=32 * 1024 * 1024),
        cost_estimate=pl.CostEstimate(
            flops=2 * depth * rows * 128 * len(groups),
            bytes_accessed=512 * rows * len(groups),
            transcendentals=0,
        ),
    )(
        pltpu.with_memory_space_constraint(cotangent, pltpu.HBM),
        pltpu.with_memory_space_constraint(tokens, pltpu.HBM),
    )


def updated(grad, master, moment1, moment2):
    first = 0.9 * moment1 + 0.1 * grad
    second = 0.95 * moment2 + 0.05 * grad * grad
    update = first / bias_first / (jnp.sqrt(second / bias_second) + 1e-08)
    return master - 0.05 * (update + 0.1 * master), first, second


def rep_grad(own, other, at):
    rep = lax.axis_index("rep")
    core, y_lo = lax.rem(rep, 2), rep // 2
    index = y_lo if at // 2 == 0 else 1 - y_lo
    piece = jnp.where(core == at % 2, own[index], other[index])
    return piece.T.astype(jnp.float32)


def adam_body(own, other, master, moment1, moment2, selector, *refs):
    outgoing, outs, weight, kept, sem = refs[0], refs[1:4], refs[4], refs[5:8], refs[8]
    copies = []
    for at in range(4):
        rows = slice(at * 128, (at + 1) * 128)
        values = updated(rep_grad(own, other, at), master[rows], moment1[rows], moment2[rows])
        weight[rows] = values[0].astype(jnp.bfloat16)
        for k in range(3):
            kept[k][rows] = values[k]
            copy = pltpu.make_async_copy(
                kept[k].at[pl.ds(at * 128, 128)], outs[k].at[pl.ds(at * 128, 128)], sem.at[k, at]
            )
            copy.start()
            copies.append(copy)
    chosen = jnp.dot(selector[...], weight[...], preferred_element_type=jnp.float32)
    outgoing[...] = chosen.astype(jnp.bfloat16).reshape(outgoing.shape)
    for copy in copies:
        copy.wait()


def adam(own, other, master, moment1, moment2, selector):
    rows, columns = master.shape
    size = rows * columns
    vmem = pl.BlockSpec(memory_space=pltpu.VMEM)
    slots = (selector.shape[0] // BLOCK_ROWS, BLOCK_ROWS, columns)
    outgoing, *state = pl.pallas_call(
        adam_body,
        out_shape=[jax.ShapeDtypeStruct(slots, jnp.bfloat16)]
        + [jax.ShapeDtypeStruct((rows, columns), jnp.float32)] * 3,
        in_specs=[vmem] * 6,
        out_specs=[vmem] + [pl.BlockSpec(memory_space=pl.ANY)] * 3,
        scratch_shapes=[pltpu.VMEM((rows, columns), jnp.bfloat16)]
        + [pltpu.VMEM((rows, columns), jnp.float32)] * 3
        + [pltpu.SemaphoreType.DMA((3, 4))],
        compiler_params=pltpu.CompilerParams(vmem_limit_bytes=16 * 1024 * 1024),
        cost_estimate=pl.CostEstimate(
            flops=20 * size, bytes_accessed=26 * size, transcendentals=0
        ),
    )(own, other, master, moment1, moment2, selector)
    return outgoing, state


def after(value, *earlier):
    return lax.optimization_barrier((value, *earlier))[0]


def combine_body(plan, *refs):
    outs = refs[len(refs) - len(plan) :]
    for out, segments in zip(outs, plan):
        begin = 0
        for rows, terms in segments:
            chunk = next(size for size in (768, 512, rows) if rows % size == 0)

            def one(step, carry, begin=begin, terms=terms, chunk=chunk, out=out):
                total = 0.0
                for source, start in terms:
                    at = pl.multiple_of(start + step * chunk, 16)
                    total = total + refs[source][pl.ds(at, chunk)].astype(jnp.float32)
                at = pl.multiple_of(begin + step * chunk, 16)
                out[pl.ds(at, chunk)] = total.astype(jnp.bfloat16)
                return carry

            lax.fori_loop(0, rows // chunk, one, 0)
            begin += rows


def combine(inputs, plan, flops=0):
    vmem = pl.BlockSpec(memory_space=pltpu.VMEM)
    sizes = [sum(rows for rows, _ in segments) for segments in plan]
    return pl.pallas_call(
        functools.partial(combine_body, plan),
        out_shape=[pltpu.VMEM((size, 128), jnp.bfloat16) for size in sizes],
        in_specs=[vmem] * len(inputs),
        out_specs=[vmem] * len(plan),
        compiler_params=pltpu.CompilerParams(
            vmem_limit_bytes=256 * (sum(sizes) + sum(value.shape[0] for value in inputs)) + 2**21
        ),
        cost_estimate=pl.CostEstimate(flops=flops, bytes_accessed=0, transcendentals=0),
    )(*inputs)


def total(inputs):
    rows = inputs[0].shape[0]
    return combine(inputs, [[(rows, [(k, 0) for k in range(len(inputs))])]])[0]


def exchanged(sums, stage):
    stay, far, even, odd = sums
    return [
        stay,
        send(even, swap_pairs(0, stage)),
        send(odd, swap_pairs(1, stage)),
        send(far, far_pairs(stage)),
    ]


def summed(tokens, cotangent, early):
    columns = cotangent.shape[1]
    other = split_sums(tokens, cotangent, [(1, 0, True), (1, 1, True)])
    own = split_sums(tokens, after(cotangent, *other), [(0, 0, True), (0, 1, True)])
    beside = [send(value, rep_pairs(1)) for value in other]
    last = []
    came = []
    for odd in range(2):
        last = [total([own[odd], after(beside[odd], *last)])]
        came.append(send(last[0], swap_pairs(odd)))

    both = split_sums(
        tokens, after(cotangent, *last), [(side, half, False) for side in (1, 0) for half in range(2)]
    )
    beside = [send(value, rep_pairs(1)) for value in both[:4]]

    rows = 8 * columns
    half_sums = []
    for odd, flops in ((0, 2 * 10**10), (1, 10**11)):
        half_sums += combine(
            [after(both[5 + 2 * odd], *half_sums), came[odd]],
            [[(rows, [(0, 0), (1, rows)])]],
            flops=flops,
        )
    sent = combine(
        [*half_sums, beside[1], beside[3]],
        [[(rows, [(odd, 0), (2 + odd, 0)])] for odd in range(2)],
    )
    got = [send(sent[odd], swap_pairs(1 - odd)) for odd in range(2)]
    near = combine(
        [both[4], both[6], after(beside[0], *sent), beside[2], *came],
        [[(rows, [(odd, 0), (2 + odd, 0), (4 + odd, 0)])] for odd in range(2)],
    )

    rows = 4 * columns
    sums = []
    for odd in range(2):
        sums += combine(
            [near[odd], after(got[odd], early)], [[(rows, [(0, at), (1, at)])] for at in (0, rows)]
        )
    sums = combine(
        exchanged(sums, 1),
        [[(columns, [(k, at * columns) for k in range(SIDE)])] for at in range(SIDE)],
    )
    return total(exchanged(sums, 2))


def select_body(capacity, fsdp_count, owner, selector):
    blocks = owner.shape[0] // fsdp_count
    shape = (blocks, blocks)
    first = pl.multiple_of(lax.axis_index("fsdp") * blocks, blocks)
    mine = owner[pl.ds(first, blocks)].reshape(1, blocks)
    by_lane = jnp.broadcast_to(mine, shape)
    earlier = lax.broadcasted_iota(jnp.int32, shape, 0) < lax.broadcasted_iota(jnp.int32, shape, 1)
    same = jnp.where(by_lane.T == by_lane, 1.0, 0.0)
    rank = jnp.sum(jnp.where(earlier, same, 0.0), axis=0, keepdims=True)
    slot = (mine % fsdp_count * capacity).astype(jnp.float32) + rank
    slot = jnp.where(mine // fsdp_count == lax.axis_index("rep"), slot, -1.0)
    rows = blocks * BLOCK_ROWS
    block = lax.broadcasted_iota(jnp.int32, (blocks, rows), 0)
    row = lax.broadcasted_iota(jnp.int32, (blocks, rows), 1)
    spread = jnp.where(row // BLOCK_ROWS == block, 1.0, 0.0).astype(jnp.bfloat16)
    slot = jnp.dot(
        jnp.broadcast_to(slot, (16, blocks)).astype(jnp.bfloat16),
        spread,
        preferred_element_type=jnp.float32,
    )[:1]
    shape = selector.shape
    slot_row = lax.broadcasted_iota(jnp.int32, shape, 0)
    row = lax.broadcasted_iota(jnp.int32, shape, 1)
    at_slot = (slot_row // BLOCK_ROWS).astype(jnp.float32) == slot
    at_row = slot_row % BLOCK_ROWS == row % BLOCK_ROWS
    selector[...] = jnp.where(jnp.logical_and(at_slot, at_row), 1.0, 0.0).astype(jnp.bfloat16)


def select_blocks(owner, capacity, fsdp_count):
    vmem = pl.BlockSpec(memory_space=pltpu.VMEM)
    shape = (fsdp_count * capacity * BLOCK_ROWS, owner.shape[0] // fsdp_count * BLOCK_ROWS)
    return pl.pallas_call(
        functools.partial(select_body, capacity, fsdp_count),
        out_shape=jax.ShapeDtypeStruct(shape, jnp.bfloat16),
        in_specs=[vmem],
        out_specs=vmem,
        compiler_params=pltpu.CompilerParams(vmem_limit_bytes=8 * 1024 * 1024),
        cost_estimate=pl.CostEstimate(flops=0, bytes_accessed=0, transcendentals=0),
    )(owner)


def per_device(tokens, cotangent, master, moment1, moment2, owner):
    fsdp_count = lax.axis_size("fsdp")
    rep_count = lax.axis_size("rep")
    shard_rows = master.shape[0]
    columns = master.shape[1]
    local_blocks = shard_rows // BLOCK_ROWS
    capacity = 2 * local_blocks // (rep_count * fsdp_count)
    selector = select_blocks(owner, capacity, fsdp_count)
    mine = summed(tokens, cotangent, selector)
    beside = send(mine, rep_pairs(2))
    own = jnp.stack([mine, beside])
    other = send(own, rep_pairs(1))
    outgoing, state = adam(own, other, master, moment1, moment2, selector)
    outgoing = outgoing.reshape(fsdp_count, capacity, BLOCK_ROWS, columns)
    received = lax.all_to_all(outgoing, "fsdp", split_axis=0, concat_axis=0, tiled=True)
    upload = received.reshape(fsdp_count * capacity, BLOCK_ROWS, columns)
    return (*state, upload)


def solution(mesh):
    placed = (
        P(("rep", "fsdp"), None),
        P(("rep", "fsdp"), None),
        P("fsdp", None),
        P("fsdp", None),
        P("fsdp", None),
        P(),
    )
    return jax.shard_map(
        per_device,
        mesh=mesh,
        in_specs=placed,
        out_specs=(
            P("fsdp", None),
            P("fsdp", None),
            P("fsdp", None),
            P(("rep", "fsdp"), None, None),
        ),
        check_vma=False,
    )
```
